32 devices in a mesh: shot: 2 (over y), gx: 16 (over z, x, core).
Axes of the slice: x: 2, y: 2, z: 4, core: 2. Of those that a mesh axis runs over, the one named last changes fastest.
Arguments:
- wave_now: float32 [4, 128, 16, 128], P('shot', 'gx'), parts along dimension 0, may hold values from -6 to 6
- wave_prev: float32 [4, 128, 16, 128], P('shot', 'gx'), parts along dimension 0, may hold values from -6 to 6
- speed_term: float32 [128, 16, 128], P('gx'), may hold values from 0.02 to 0.07
- thomsen_epsilon: float32 [128, 16, 128], P('gx'), may hold values from 0.15 to 0.35
- thomsen_delta: float32 [128, 16, 128], P('gx'), may hold values from 0 to 0.1
- tilt_angle: float32 [128, 16, 128], P('gx'), may hold values from -3.140625 to 3.140625
- source_store: bfloat16 [4, 4, 128, 16, 128], P('shot', None, None, 'gx'), parts along dimension 0, may hold values from -6 to 6
- receiver_row: int32 [256], P('shot'), parts along dimension 0, may hold values from 0 to 127
- receiver_column: int32 [256], P('shot'), parts along dimension 0, may hold values from 0 to 15
- receiver_traces: float32 [8, 128], P('shot'), parts along dimension 0, may hold values from -12 to 12
- angle_table: int32 [32], replicated, may hold values from 0 to 7, as said below
Outputs:
- angle_images: bfloat16 [16, 128, 16, 128], P('shot', 'gx'), parts along dimension 0
- wave_final: float32 [4, 128, 16, 128], P('shot', 'gx'), parts along dimension 0
The draws below stay inside these ranges and needn't reach their ends.
There are 2 independent parts, one for each index of `shot`. The reference program is written for one: setup_inputs(seed, part) draws one part's arguments, and reference() takes and returns one part's arrays. A program takes and returns all parts, laid end to end along the dimension named above; an argument that names none is the same for every part. Nothing has to cross between parts.
Inputs may be any that keep to these rules, and one draw needn't show every extreme that they name: angle_table is non-decreasing: angle_table[f] <= angle_table[f+1] for every fine bin f, and every one of the 8 angle images is named by at least one fine bin.
All inputs are finite; a program needn't handle non-finite values.
Results may differ from the reference program's by a relative error of at most 0.001.
Values may be sent and summed in bfloat16 or wider, within the bound.
A program may use at most 128 MiB of HBM per device.

```python
import jax
import jax.numpy as jnp
from jax import lax

NZ = 128
STEPS = 4
IMAGE_EVERY = 2
NBIN = 8
FINE = 32
REC_DEPTH = 2
NSNAP = 2
NX = 128
NY = 16
NREC = 128


def draw_angle_table(key, part):
    boundary = jax.random.permutation(key, FINE - 1)[:NBIN - 1] + 1
    positions = jnp.arange(FINE, dtype=jnp.int32)
    return jnp.sum((boundary[None, :] <= positions[:, None]).astype(jnp.int32), axis=1).astype(jnp.int32)


def touch_ends(entries, own_key, smallest, high):
    longest = entries.shape.index(max(entries.shape))
    spots = []
    for shift in (0, 1):
        where = [jax.random.randint(jax.random.fold_in(own_key, axis), (), 0, length) for axis, length in enumerate(entries.shape)]
        where[longest] = (where[longest] + shift) % entries.shape[longest]
        spots.append(tuple(where))
    return entries.at[spots[0]].set(smallest).at[spots[1]].set(high)


def block_scale(key, dims, shards, low, largest):
    def one(dim, parts):
        draws = jax.random.uniform(jax.random.fold_in(jax.random.fold_in(key, 6), dim), (parts,), jnp.float32, low / len(shards), largest / len(shards))
        return jnp.repeat(jnp.exp(draws), dims[dim] // parts).reshape((-1,) + (1,) * (len(dims) - dim - 1))

    factor_of = one(*shards[0])
    for cut in shards[1:]:
        factor_of = factor_of * one(*cut)
    return factor_of


def gaussian(key, shape, deviation, most, split=(), kind=jnp.bfloat16):
    drawn = deviation * jax.random.normal(key, shape, jnp.float32)
    if split:
        drawn = drawn * block_scale(key, shape, split, -0.22, 0.18)
    return jnp.clip(drawn, -most, most).astype(kind)


def setup_inputs(seed: int = 0, part: int = 0) -> dict:
    keys = jax.random.split(jax.random.key(seed), 12)
    part_keys = jax.random.split(jax.random.fold_in(keys[11], part), 12)
    return {
        "wave_now": gaussian(part_keys[0], (2, NX, NY, NZ), 1.0, 6.0, ((1, 16),), jnp.float32),
        "wave_prev": gaussian(part_keys[1], (2, NX, NY, NZ), 1.0, 6.0, ((1, 16),), jnp.float32),
        "speed_term": jnp.clip(0.02 + 0.05 * jax.random.uniform(keys[2], (NX, NY, NZ), jnp.float32) ** block_scale(keys[2], (NX, NY, NZ), ((0, 16),), -0.2, 0.2), 0.02, 0.07),
        "thomsen_epsilon": jnp.clip(0.15 + 0.19999999 * jax.random.uniform(keys[3], (NX, NY, NZ), jnp.float32) ** block_scale(keys[3], (NX, NY, NZ), ((0, 16),), -0.2, 0.2), 0.15, 0.35),
        "thomsen_delta": jnp.clip(0.1 * jax.random.uniform(keys[4], (NX, NY, NZ), jnp.float32) ** block_scale(keys[4], (NX, NY, NZ), ((0, 16),), -0.2, 0.2), 0.0, 0.1),
        "tilt_angle": jnp.clip(jax.random.uniform(keys[5], (NX, NY, NZ), jnp.float32, -3.140625, 3.140625), -3.140625, 3.140625),
        "source_store": gaussian(part_keys[6], (NSNAP, 4, NX, NY, NZ), 1.0, 6.0, ((3, 16),)),
        "receiver_row": touch_ends(jax.random.randint(part_keys[7], (NREC,), 0, NX), jax.random.fold_in(part_keys[7], 1), 0, NX - 1).astype(jnp.int32),
        "receiver_column": touch_ends(jax.random.randint(part_keys[8], (NREC,), 0, NY), jax.random.fold_in(part_keys[8], 1), 0, NY - 1).astype(jnp.int32),
        "receiver_traces": gaussian(part_keys[9], (STEPS, NREC), 2.0, 12.0, (), jnp.float32),
        "angle_table": draw_angle_table(jax.random.fold_in(keys[11], 71), part),
    }


second_coeffs = (-205.0 / 72.0, 8.0 / 5.0, -1.0 / 5.0, 8.0 / 315.0, -1.0 / 560.0)
first_coeffs = (4.0 / 5.0, -1.0 / 5.0, 4.0 / 105.0, -1.0 / 280.0)
stencil_reach = 4

def window(array_in, direction, begin_at, extent):
    return lax.slice_in_dim(array_in, begin_at, begin_at + extent, axis=direction)

def moved(field, direction, offset):
    length = field.shape[direction]
    shape = list(field.shape)
    shape[direction] = abs(offset)
    zeros = jnp.zeros(tuple(shape), field.dtype)
    if offset > 0:
        return jnp.concatenate([lax.slice_in_dim(field, offset, length, axis=direction), zeros], axis=direction)
    return jnp.concatenate([zeros, lax.slice_in_dim(field, 0, length + offset, axis=direction)], axis=direction)

def second_along(field, direction):
    summed = second_coeffs[0] * field
    for offset in range(1, 5):
        summed = summed + second_coeffs[offset] * (moved(field, direction, offset) + moved(field, direction, -offset))
    return summed

def first_along(field, direction):
    summed = first_coeffs[0] * (moved(field, direction, 1) - moved(field, direction, -1))
    for offset in range(2, 5):
        summed = summed + first_coeffs[offset - 1] * (moved(field, direction, offset) - moved(field, direction, -offset))
    return summed

def second_diff(padded, direction, extent):
    summed = second_coeffs[0] * window(padded, direction, stencil_reach, extent)
    for offset in range(1, 5):
        summed = summed + second_coeffs[offset] * (window(padded, direction, stencil_reach + offset, extent) + window(padded, direction, stencil_reach - offset, extent))
    return summed

def first_diff(padded, direction, extent):
    summed = first_coeffs[0] * (window(padded, direction, stencil_reach + 1, extent) - window(padded, direction, stencil_reach - 1, extent))
    for offset in range(2, 5):
        summed = summed + first_coeffs[offset - 1] * (window(padded, direction, stencil_reach + offset, extent) - window(padded, direction, stencil_reach - offset, extent))
    return summed

def advance(padded, earlier, medium, traces_now, receiver_row, receiver_column, first_row):
    extent_x = earlier.shape[1]
    extent_y = earlier.shape[2]
    speed, epsilon, thomsen, tilt = medium
    second_x = second_diff(padded, 1, extent_x)
    inner_rows = padded[:, 4:-4]
    second_y = second_along(inner_rows[0], 1)
    second_z = second_along(inner_rows, 3)
    slope_z_all = first_along(padded, 3)
    mixed = first_diff(slope_z_all, 1, extent_x)
    slope_x = first_diff(padded[0], 0, extent_x)
    slope_y = first_along(inner_rows[0], 1)
    slope_z = slope_z_all[0, 4:-4]
    cosine = jnp.cos(tilt)
    sine = jnp.sin(tilt)
    rotated = cosine * cosine * second_z + sine * sine * second_x + 2.0 * sine * cosine * mixed
    across_p = second_x[0] + second_y + second_z[0] - rotated[0]
    ratio = jnp.sqrt(1.0 + 2.0 * thomsen)
    centre = inner_rows
    p_next = 2.0 * centre[0] - earlier[0] + speed * ((1.0 + 2.0 * epsilon) * across_p + ratio * rotated[1])
    q_next = 2.0 * centre[1] - earlier[1] + speed * (ratio * across_p + rotated[1])
    local_row = receiver_row - first_row
    inside = (local_row >= 0) & (local_row < extent_x)
    flat_index = jnp.where(inside, local_row * extent_y + receiver_column, extent_x * extent_y)
    plane = jnp.zeros((extent_x * extent_y,), jnp.float32).at[flat_index].add(traces_now, mode='drop')
    p_next = p_next.at[:, :, REC_DEPTH].add(plane.reshape(extent_x, extent_y))
    return (jnp.stack([p_next, q_next]), (slope_x, slope_y, slope_z))

def angle_image(snapshot, wave_field, earlier_field, slopes, selector):
    fine_count = selector.shape[1]
    rate = wave_field - earlier_field
    flux_x = -rate * slopes[0]
    flux_y = -rate * slopes[1]
    flux_z = -rate * slopes[2]
    inner = snapshot[1] * flux_x + snapshot[2] * flux_y + snapshot[3] * flux_z
    lengths = jnp.sqrt(snapshot[1] * snapshot[1] + snapshot[2] * snapshot[2] + snapshot[3] * snapshot[3]) * jnp.sqrt(flux_x * flux_x + flux_y * flux_y + flux_z * flux_z)
    cosine = inner / jnp.maximum(lengths, 1.0)
    scaled = (cosine + 1.0) * (0.5 * (fine_count - 1))
    centres = jnp.arange(fine_count, dtype=jnp.float32).reshape((fine_count,) + (1,) * scaled.ndim)
    weights = jnp.maximum(0.0, 1.0 - jnp.abs(scaled[None] - centres)) * (snapshot[0] * wave_field)[None]
    summed = jnp.dot(selector, weights.reshape(fine_count, -1), precision=lax.Precision.HIGHEST, preferred_element_type=jnp.float32)
    return summed.reshape((selector.shape[0],) + wave_field.shape)

def sliced_image(snapshot, current, earlier, slopes, selector):
    inputs = (jnp.moveaxis(snapshot, 1, 0), current, earlier, slopes[0], slopes[1], slopes[2])

    def one_slab(pieces):
        return angle_image(pieces[0], pieces[1], pieces[2], (pieces[3], pieces[4], pieces[5]), selector)
    return jnp.moveaxis(lax.map(one_slab, inputs), 1, 0)

def reference(wave_now, wave_prev, speed_term, thomsen_epsilon, thomsen_delta, tilt_angle, source_store, receiver_row, receiver_column, receiver_traces, angle_table):
    medium = (speed_term, thomsen_epsilon, thomsen_delta, tilt_angle)
    selector = (angle_table[None, :] == jnp.arange(NBIN, dtype=jnp.int32)[:, None]).astype(jnp.float32)
    current = wave_now
    earlier = wave_prev
    images = jnp.zeros((NBIN, NX, NY, NZ), jnp.float32)
    for time_step in range(STEPS):
        padded = jnp.pad(current, ((0, 0), (4, 4), (0, 0), (0, 0)))
        following, slopes = advance(padded, earlier, medium, receiver_traces[time_step], receiver_row, receiver_column, 0)
        if time_step % IMAGE_EVERY == IMAGE_EVERY - 1:
            snapshot = source_store[time_step // IMAGE_EVERY].astype(jnp.float32)
            images = images + sliced_image(snapshot, current[0], earlier[0], slopes, selector)
        earlier = current
        current = following
    return (images.astype(jnp.bfloat16), current)
```

```python
import functools

import jax
import jax.numpy as jnp
from jax import lax
from jax.experimental import pallas as pl
from jax.experimental.pallas import tpu as pltpu
from jax.sharding import PartitionSpec as P

STEPS = 4
IMAGE_EVERY = 2
NBIN = 8
FINE = 32
REC_DEPTH = 2
REACH = 4
GROUP = 4

second_coeffs = (-205.0 / 72.0, 8.0 / 5.0, -1.0 / 5.0, 8.0 / 315.0, -1.0 / 560.0)
first_coeffs = (4.0 / 5.0, -1.0 / 5.0, 4.0 / 105.0, -1.0 / 280.0)
MESH = pl.DeviceIdType.MESH


def shifted_pairs(f, axis):
    size = f.shape[axis]
    place = lax.broadcasted_iota(jnp.int32, f.shape, axis)
    pairs = []
    for k in range(1, REACH + 1):
        ahead = jnp.where(place < size - k, pltpu.roll(f, size - k, axis), 0.0)
        behind = jnp.where(place >= k, pltpu.roll(f, k, axis), 0.0)
        pairs.append((ahead, behind))
    return pairs


def second_of(f, pairs):
    total = second_coeffs[0] * f
    for k, (ahead, behind) in enumerate(pairs):
        total = total + second_coeffs[k + 1] * (ahead + behind)
    return total


def first_of(pairs):
    total = None
    for k, (ahead, behind) in enumerate(pairs):
        term = first_coeffs[k] * (ahead - behind)
        total = term if total is None else total + term
    return total


def row_pairs(ref, lead, start):
    return [
        (
            ref[lead + (pl.ds(start + REACH + k, GROUP),)],
            ref[lead + (pl.ds(start + REACH - k, GROUP),)],
        )
        for k in range(1, REACH + 1)
    ]


def kernel(
    n,
    now_hbm, prev_hbm, speed_hbm, eps_hbm, delta_hbm, tilt_hbm, source_hbm,
    rows_ref, cols_ref, traces_ref, table_ref,
    images_ref, final_ref,
    pad, prev, med, coef, source, staged, arrived, snap, slopes, aim, inject, base, slope_z,
    in_sem, halo_send, halo_recv, all_send, all_recv,
):
    me = lax.axis_index("gx")
    nx, ny, nz = prev.shape[1:]
    local_ny = source.shape[2]
    has_left, has_right = me > 0, me < n - 1
    left, right = lax.rem(me + n - 1, n), lax.rem(me + 1, n)
    own = pl.ds(REACH, nx)
    far = REACH + nx

    barrier = pltpu.get_barrier_semaphore()

    def greet(k, carry):
        pl.semaphore_signal(
            barrier, inc=1, device_id={"gx": lax.rem(me + k, n)}, device_id_type=MESH
        )
        return carry

    lax.fori_loop(1, n, greet, 0)

    loads = [
        pltpu.make_async_copy(source_hbm, source, in_sem.at[0]),
        pltpu.make_async_copy(tilt_hbm, med.at[0], in_sem.at[1]),
        pltpu.make_async_copy(speed_hbm, med.at[1], in_sem.at[2]),
        pltpu.make_async_copy(eps_hbm, med.at[2], in_sem.at[3]),
        pltpu.make_async_copy(delta_hbm, med.at[3], in_sem.at[4]),
        pltpu.make_async_copy(now_hbm, pad.at[0, :, own], in_sem.at[5]),
        pltpu.make_async_copy(prev_hbm, prev, in_sem.at[6]),
    ]
    for load in loads:
        load.start()

    def halo_left(t):
        source_of = now_hbm.at[:, pl.ds(0, REACH)] if t == 0 else pad.at[t, :, pl.ds(REACH, REACH)]
        return pltpu.make_async_remote_copy(
            src_ref=source_of,
            dst_ref=pad.at[t, :, pl.ds(far, REACH)],
            send_sem=halo_send.at[t, 0],
            recv_sem=halo_recv.at[t, 1],
            device_id={"gx": left},
            device_id_type=MESH,
        )

    def halo_right(t):
        source_of = (
            now_hbm.at[:, pl.ds(nx - REACH, REACH)] if t == 0 else pad.at[t, :, pl.ds(nx, REACH)]
        )
        return pltpu.make_async_remote_copy(
            src_ref=source_of,
            dst_ref=pad.at[t, :, pl.ds(0, REACH)],
            send_sem=halo_send.at[t, 1],
            recv_sem=halo_recv.at[t, 0],
            device_id={"gx": right},
            device_id_type=MESH,
        )

    def block_to(j, k, target, slot):
        return pltpu.make_async_remote_copy(
            src_ref=staged.at[j, target],
            dst_ref=arrived.at[j, pl.ds(slot * local_ny, local_ny)],
            send_sem=all_send.at[j, k],
            recv_sem=all_recv.at[j, k],
            device_id={"gx": target},
            device_id_type=MESH,
        )

    def send_blocks(j):
        def send(k, carry):
            block_to(j, k, lax.rem(me + k, n), me).start()
            return carry

        lax.fori_loop(1, n, send, 0)
        arrived[j, pl.ds(me * local_ny, local_ny)] = staged[j, me]

    def take_blocks(j):
        def take(k, carry):
            block_to(j, k, lax.rem(me + k, n), lax.rem(me + n - k, n)).wait_recv()
            return carry

        lax.fori_loop(1, n, take, 0)

    def sent_blocks(j):
        def sent(k, carry):
            block_to(j, k, lax.rem(me + k, n), me).wait_send()
            return carry

        lax.fori_loop(1, n, sent, 0)

    pl.semaphore_wait(barrier, n - 1)

    @pl.when(has_left)
    def _():
        halo_left(0).start()

    @pl.when(has_right)
    def _():
        halo_right(0).start()

    for t in range(STEPS):
        @pl.when(me == 0)
        def _():
            pad[t, :, pl.ds(0, REACH)] = jnp.zeros((2, REACH, ny, nz), jnp.float32)

        @pl.when(me == n - 1)
        def _():
            pad[t, :, pl.ds(far, REACH)] = jnp.zeros((2, REACH, ny, nz), jnp.float32)

    loads[0].wait()
    for j in range(source.shape[0]):
        for y in range(local_ny):
            for c in range(4):
                whole = source[j, c, y].astype(jnp.float32).reshape(n, nx, nz)
                snap[c, pl.ds(0, n)] = whole
            joined = jnp.concatenate([snap[c, pl.ds(0, n)] for c in range(4)], axis=1)
            staged[j, :, y] = joined.astype(jnp.bfloat16)
        if j == 0:
            send_blocks(0)

    for load in loads[1:5]:
        load.wait()
    for i in range(0, nx, GROUP):
        rows = pl.ds(i, GROUP)
        tilt = med[0, rows]
        cosine = jnp.cos(tilt)
        sine = jnp.sin(tilt)
        speed = med[1, rows]
        ratio = jnp.sqrt(1.0 + 2.0 * med[3, rows])
        coef[0, rows] = cosine * cosine
        coef[1, rows] = sine * sine
        coef[2, rows] = 2.0 * sine * cosine
        coef[3, rows] = speed * (1.0 + 2.0 * med[2, rows])
        coef[4, rows] = speed * ratio
        coef[5, rows] = speed

    first_row = me * nx
    at_column = cols_ref[...] == lax.broadcasted_iota(jnp.int32, (ny, cols_ref.shape[1]), 0)
    at_depth = lax.broadcasted_iota(jnp.int32, (ny, nz), 1) == REC_DEPTH

    def one_row(x, carry):
        here = jnp.where(rows_ref[...] == first_row + x, traces_ref[...], 0.0)
        for t in range(STEPS):
            summed = jnp.sum(
                jnp.where(at_column, here[t : t + 1], 0.0), axis=1, keepdims=True
            )
            inject[t, x] = jnp.where(at_depth, summed, 0.0)
        return carry

    lax.fori_loop(0, nx, one_row, 0)

    for load in loads[5:]:
        load.wait()

    def before(t):
        imaging = t % IMAGE_EVERY == IMAGE_EVERY - 1
        for i in range(0, nx, GROUP):
            rows = pl.ds(i, GROUP)
            p = pad[t, 0, pl.ds(REACH + i, GROUP)]
            q = pad[t, 1, pl.ds(REACH + i, GROUP)]
            p_old = prev[0, rows] if t == 0 else pad[t - 1, 0, pl.ds(REACH + i, GROUP)]
            q_old = prev[1, rows] if t == 0 else pad[t - 1, 1, pl.ds(REACH + i, GROUP)]
            pairs = shifted_pairs(p, 2)
            slope = first_of(pairs)
            slope_z[0, pl.ds(REACH + i, GROUP)] = slope
            p_zz = second_of(p, pairs)
            pairs = shifted_pairs(q, 2)
            slope_z[1, pl.ds(REACH + i, GROUP)] = first_of(pairs)
            q_zz = second_of(q, pairs)
            pairs = shifted_pairs(p, 1)
            p_yy = second_of(p, pairs)
            if imaging:
                j = t // IMAGE_EVERY
                slopes[j, 1, rows] = first_of(pairs)
                slopes[j, 2, rows] = slope
            across = coef[1, rows] * p_zz + p_yy
            rotated = coef[0, rows] * q_zz
            base[0, rows] = (
                2.0 * p - p_old + inject[t, rows]
                + (coef[3, rows] * across + coef[4, rows] * rotated)
            )
            base[1, rows] = (
                2.0 * q - q_old + (coef[4, rows] * across + coef[5, rows] * rotated)
            )

    def after(t):
        imaging = t % IMAGE_EVERY == IMAGE_EVERY - 1
        last = t == STEPS - 1

        @pl.when(has_left)
        def _():
            halo_left(t).wait_send()
            halo_right(t).wait_recv()

        @pl.when(has_right)
        def _():
            halo_right(t).wait_send()
            halo_left(t).wait_recv()

        for start in (0, far):
            for f in range(2):
                rows = pl.ds(start, REACH)
                slope_z[f, rows] = first_of(shifted_pairs(pad[t, f, rows], 2))
        for i in range(0, nx, GROUP):
            rows = pl.ds(i, GROUP)
            middle = pl.ds(REACH + i, GROUP)
            pairs = row_pairs(pad, (t, 0), i)
            p_xx = second_of(pad[t, 0, middle], pairs)
            if imaging:
                slopes[t // IMAGE_EVERY, 0, rows] = first_of(pairs)
            q_xx = second_of(pad[t, 1, middle], row_pairs(pad, (t, 1), i))
            p_xz = first_of(row_pairs(slope_z, (0,), i))
            q_xz = first_of(row_pairs(slope_z, (1,), i))
            across = coef[0, rows] * p_xx - coef[2, rows] * p_xz
            rotated = coef[1, rows] * q_xx + coef[2, rows] * q_xz
            p_new = base[0, rows] + (coef[3, rows] * across + coef[4, rows] * rotated)
            q_new = base[1, rows] + (coef[4, rows] * across + coef[5, rows] * rotated)
            if last:
                final_ref[0, rows] = p_new
                final_ref[1, rows] = q_new
            else:
                pad[t + 1, 0, middle] = p_new
                pad[t + 1, 1, middle] = q_new
                if i == 0:
                    @pl.when(has_left)
                    def _():
                        halo_left(t + 1).start()

                if i + GROUP == nx:
                    @pl.when(has_right)
                    def _():
                        halo_right(t + 1).start()

    def angles(j):
        t = j * IMAGE_EVERY + IMAGE_EVERY - 1
        take_blocks(j)
        blocks = arrived[j].astype(jnp.float32)
        for c in range(4):
            snap[c] = blocks[:, c * nx : (c + 1) * nx]
        for x in range(nx):
            s, fx, fy, fz = (
                snap.at[c].reshape(ny * nx, nz)[pl.ds(x, ny, stride=nx), :] for c in range(4)
            )
            p = pad[t, 0, REACH + x]
            rate = p - pad[t - 1, 0, REACH + x]
            gx = -rate * slopes[j, 0, x]
            gy = -rate * slopes[j, 1, x]
            gz = -rate * slopes[j, 2, x]
            inner = fx * gx + fy * gy + fz * gz
            lengths = jnp.sqrt(fx * fx + fy * fy + fz * fz) * jnp.sqrt(gx * gx + gy * gy + gz * gz)
            cosine = inner / jnp.maximum(lengths, 1.0)
            aim[j, 0, x] = (cosine + 1.0) * (0.5 * (FINE - 1))
            aim[j, 1, x] = s * p

    before(0)
    after(0)
    send_blocks(1)
    before(1)
    after(1)
    before(2)
    after(2)
    before(3)
    angles(0)
    after(3)
    angles(1)

    table = table_ref[...]
    lower = [
        jnp.sum((table < b).astype(jnp.float32), axis=1, keepdims=True) for b in range(NBIN + 1)
    ]
    for x in range(nx):
        uses = [(aim[j, 0, x], aim[j, 1, x]) for j in range(STEPS // IMAGE_EVERY)]
        above = [jnp.clip(u - lower[0] + 1.0, 0.0, 1.0) for u, _ in uses]
        for b in range(NBIN):
            beyond = [jnp.clip(u - lower[b + 1] + 1.0, 0.0, 1.0) for u, _ in uses]
            total = None
            for (_, w), low, high in zip(uses, above, beyond):
                term = (low - high) * w
                total = term if total is None else total + term
            images_ref[b, x] = total.astype(jnp.bfloat16)
            above = beyond
    sent_blocks(0)
    sent_blocks(1)


def local(
    n,
    wave_now,
    wave_prev,
    speed_term,
    thomsen_epsilon,
    thomsen_delta,
    tilt_angle,
    source_store,
    receiver_row,
    receiver_column,
    receiver_traces,
    angle_table,
):
    fields, nx, ny, nz = wave_now.shape
    snaps, parts, whole_x, local_ny, _ = source_store.shape
    padded_x = nx + 2 * REACH
    f32, bf16 = jnp.float32, jnp.bfloat16
    hbm = pl.BlockSpec(memory_space=pl.ANY)
    vmem = pl.BlockSpec(memory_space=pltpu.VMEM)
    return pl.pallas_call(
        functools.partial(kernel, n),
        out_shape=(
            jax.ShapeDtypeStruct((NBIN, nx, ny, nz), bf16),
            jax.ShapeDtypeStruct((fields, nx, ny, nz), f32),
        ),
        in_specs=[hbm] * 7 + [vmem] * 4,
        out_specs=(vmem, vmem),
        scratch_shapes=[
            pltpu.VMEM((STEPS, fields, padded_x, ny, nz), f32),
            pltpu.VMEM((fields, nx, ny, nz), f32),
            pltpu.VMEM((4, nx, ny, nz), f32),
            pltpu.VMEM((6, nx, ny, nz), f32),
            pltpu.VMEM((snaps, parts, local_ny, whole_x, nz), bf16),
            pltpu.VMEM((snaps, n, local_ny, parts * nx, nz), bf16),
            pltpu.VMEM((snaps, ny, parts * nx, nz), bf16),
            pltpu.VMEM((parts, ny, nx, nz), f32),
            pltpu.VMEM((snaps, 3, nx, ny, nz), f32),
            pltpu.VMEM((snaps, 2, nx, ny, nz), f32),
            pltpu.VMEM((STEPS, nx, ny, nz), f32),
            pltpu.VMEM((fields, nx, ny, nz), f32),
            pltpu.VMEM((fields, padded_x, ny, nz), f32),
            pltpu.SemaphoreType.DMA((7,)),
            pltpu.SemaphoreType.DMA((STEPS, 2)),
            pltpu.SemaphoreType.DMA((STEPS, 2)),
            pltpu.SemaphoreType.DMA((snaps, n)),
            pltpu.SemaphoreType.DMA((snaps, n)),
        ],
        compiler_params=pltpu.CompilerParams(
            collective_id=0, has_side_effects=True, vmem_limit_bytes=48 * 1024 * 1024
        ),
    )(
        wave_now,
        wave_prev,
        speed_term,
        thomsen_epsilon,
        thomsen_delta,
        tilt_angle,
        source_store.transpose(0, 1, 3, 2, 4),
        receiver_row.reshape(1, -1),
        receiver_column.reshape(1, -1),
        receiver_traces,
        angle_table.reshape(1, -1),
    )


def solution(mesh):
    placed = (
        P("shot", "gx", None, None),
        P("shot", "gx", None, None),
        P("gx", None, None),
        P("gx", None, None),
        P("gx", None, None),
        P("gx", None, None),
        P("shot", None, None, "gx", None),
        P("shot"),
        P("shot"),
        P("shot", None),
        P(),
    )
    return jax.shard_map(
        functools.partial(local, mesh.shape["gx"]),
        mesh=mesh,
        in_specs=placed,
        out_specs=(P("shot", "gx", None, None), P("shot", "gx", None, None)),
        check_vma=False,
    )
```

```python
import functools

import jax
import jax.numpy as jnp
from jax import lax
from jax.experimental import pallas as pl
from jax.experimental.pallas import tpu as pltpu
from jax.sharding import PartitionSpec as P

STEPS = 4
IMAGE_EVERY = 2
NBIN = 8
FINE = 32
REC_DEPTH = 2
REACH = 4
GROUP = 4

second_coeffs = (-205.0 / 72.0, 8.0 / 5.0, -1.0 / 5.0, 8.0 / 315.0, -1.0 / 560.0)
first_coeffs = (4.0 / 5.0, -1.0 / 5.0, 4.0 / 105.0, -1.0 / 280.0)
MESH = pl.DeviceIdType.MESH


def shifted_pairs(f, axis):
    size = f.shape[axis]
    place = lax.broadcasted_iota(jnp.int32, f.shape, axis)
    pairs = []
    for k in range(1, REACH + 1):
        ahead = jnp.where(place < size - k, pltpu.roll(f, size - k, axis), 0.0)
        behind = jnp.where(place >= k, pltpu.roll(f, k, axis), 0.0)
        pairs.append((ahead, behind))
    return pairs


def second_of(f, pairs):
    total = second_coeffs[0] * f
    for k, (ahead, behind) in enumerate(pairs):
        total = total + second_coeffs[k + 1] * (ahead + behind)
    return total


def first_of(pairs):
    total = None
    for k, (ahead, behind) in enumerate(pairs):
        term = first_coeffs[k] * (ahead - behind)
        total = term if total is None else total + term
    return total


def row_pairs(ref, lead, start):
    return [
        (
            ref[lead + (pl.ds(start + REACH + k, GROUP),)],
            ref[lead + (pl.ds(start + REACH - k, GROUP),)],
        )
        for k in range(1, REACH + 1)
    ]


def kernel(
    n,
    now_hbm, prev_hbm, speed_hbm, eps_hbm, delta_hbm, tilt_hbm, source_hbm,
    rows_hbm, cols_hbm, traces_hbm, table_hbm,
    images_ref, final_ref,
    pad, prev, med, coef, source, staged, arrived, snap, slopes, aim, inject, base, slope_z,
    rows_ref, cols_ref, traces_ref, table_ref,
    in_sem, halo_send, halo_recv, all_send, all_recv,
):
    me = lax.axis_index("gx")
    nx, ny, nz = prev.shape[1:]
    local_ny = source.shape[2]
    has_left, has_right = me > 0, me < n - 1
    left, right = lax.rem(me + n - 1, n), lax.rem(me + 1, n)
    own = pl.ds(REACH, nx)
    far = REACH + nx

    barrier = pltpu.get_barrier_semaphore()

    def greet(k, carry):
        pl.semaphore_signal(
            barrier, inc=1, device_id={"gx": lax.rem(me + k, n)}, device_id_type=MESH
        )
        return carry

    lax.fori_loop(1, n, greet, 0)

    loads = [
        pltpu.make_async_copy(source_hbm, source, in_sem.at[0]),
        pltpu.make_async_copy(tilt_hbm, med.at[0], in_sem.at[1]),
        pltpu.make_async_copy(speed_hbm, med.at[1], in_sem.at[2]),
        pltpu.make_async_copy(eps_hbm, med.at[2], in_sem.at[3]),
        pltpu.make_async_copy(delta_hbm, med.at[3], in_sem.at[4]),
        pltpu.make_async_copy(rows_hbm, rows_ref, in_sem.at[7]),
        pltpu.make_async_copy(cols_hbm, cols_ref, in_sem.at[8]),
        pltpu.make_async_copy(traces_hbm, traces_ref, in_sem.at[9]),
        pltpu.make_async_copy(table_hbm, table_ref, in_sem.at[10]),
        pltpu.make_async_copy(now_hbm, pad.at[0, :, own], in_sem.at[5]),
        pltpu.make_async_copy(prev_hbm, prev, in_sem.at[6]),
    ]
    for load in loads:
        load.start()

    def halo_left(t):
        source_of = now_hbm.at[:, pl.ds(0, REACH)] if t == 0 else pad.at[t, :, pl.ds(REACH, REACH)]
        return pltpu.make_async_remote_copy(
            src_ref=source_of,
            dst_ref=pad.at[t, :, pl.ds(far, REACH)],
            send_sem=halo_send.at[t, 0],
            recv_sem=halo_recv.at[t, 1],
            device_id={"gx": left},
            device_id_type=MESH,
        )

    def halo_right(t):
        source_of = (
            now_hbm.at[:, pl.ds(nx - REACH, REACH)] if t == 0 else pad.at[t, :, pl.ds(nx, REACH)]
        )
        return pltpu.make_async_remote_copy(
            src_ref=source_of,
            dst_ref=pad.at[t, :, pl.ds(0, REACH)],
            send_sem=halo_send.at[t, 1],
            recv_sem=halo_recv.at[t, 0],
            device_id={"gx": right},
            device_id_type=MESH,
        )

    def block_to(j, k, target, slot):
        return pltpu.make_async_remote_copy(
            src_ref=staged.at[j, target],
            dst_ref=arrived.at[j, pl.ds(slot * local_ny, local_ny)],
            send_sem=all_send.at[j, k],
            recv_sem=all_recv.at[j, k],
            device_id={"gx": target},
            device_id_type=MESH,
        )

    def send_blocks(j):
        def send(k, carry):
            block_to(j, k, lax.rem(me + k, n), me).start()
            return carry

        lax.fori_loop(1, n, send, 0)
        arrived[j, pl.ds(me * local_ny, local_ny)] = staged[j, me]

    def take_blocks(j):
        def take(k, carry):
            block_to(j, k, lax.rem(me + k, n), lax.rem(me + n - k, n)).wait_recv()
            return carry

        lax.fori_loop(1, n, take, 0)

    def sent_blocks(j):
        def sent(k, carry):
            block_to(j, k, lax.rem(me + k, n), me).wait_send()
            return carry

        lax.fori_loop(1, n, sent, 0)

    for t in range(STEPS):
        @pl.when(me == 0)
        def _():
            pad[t, :, pl.ds(0, REACH)] = jnp.zeros((2, REACH, ny, nz), jnp.float32)

        @pl.when(me == n - 1)
        def _():
            pad[t, :, pl.ds(far, REACH)] = jnp.zeros((2, REACH, ny, nz), jnp.float32)

    for load in loads[1:9]:
        load.wait()
    for i in range(0, nx, GROUP):
        rows = pl.ds(i, GROUP)
        tilt = med[0, rows]
        cosine = jnp.cos(tilt)
        sine = jnp.sin(tilt)
        speed = med[1, rows]
        ratio = jnp.sqrt(1.0 + 2.0 * med[3, rows])
        coef[0, rows] = cosine * cosine
        coef[1, rows] = sine * sine
        coef[2, rows] = 2.0 * sine * cosine
        coef[3, rows] = speed * (1.0 + 2.0 * med[2, rows])
        coef[4, rows] = speed * ratio
        coef[5, rows] = speed

    first_row = me * nx
    at_column = cols_ref[...] == lax.broadcasted_iota(jnp.int32, (ny, cols_ref.shape[1]), 0)
    at_depth = lax.broadcasted_iota(jnp.int32, (ny, nz), 1) == REC_DEPTH

    def one_row(x, carry):
        here = jnp.where(rows_ref[...] == first_row + x, traces_ref[...], 0.0)
        for t in range(STEPS):
            summed = jnp.sum(
                jnp.where(at_column, here[t : t + 1], 0.0), axis=1, keepdims=True
            )
            inject[t, x] = jnp.where(at_depth, summed, 0.0)
        return carry

    lax.fori_loop(0, nx, one_row, 0)

    pl.semaphore_wait(barrier, n - 1)

    @pl.when(has_left)
    def _():
        halo_left(0).start()

    @pl.when(has_right)
    def _():
        halo_right(0).start()

    def stage(j):
        for y in range(local_ny):
            for c in range(4):
                snap[c, pl.ds(0, n)] = source[j, c, y].astype(jnp.float32).reshape(n, nx, nz)
            joined = jnp.concatenate([snap[c, pl.ds(0, n)] for c in range(4)], axis=1)
            staged[j, :, y] = joined.astype(jnp.bfloat16)
        send_blocks(j)

    loads[0].wait()
    stage(0)
    for load in loads[9:]:
        load.wait()

    def before(t):
        imaging = t % IMAGE_EVERY == IMAGE_EVERY - 1
        for i in range(0, nx, GROUP):
            rows = pl.ds(i, GROUP)
            p = pad[t, 0, pl.ds(REACH + i, GROUP)]
            q = pad[t, 1, pl.ds(REACH + i, GROUP)]
            p_old = prev[0, rows] if t == 0 else pad[t - 1, 0, pl.ds(REACH + i, GROUP)]
            q_old = prev[1, rows] if t == 0 else pad[t - 1, 1, pl.ds(REACH + i, GROUP)]
            pairs = shifted_pairs(p, 2)
            slope = first_of(pairs)
            slope_z[0, pl.ds(REACH + i, GROUP)] = slope
            p_zz = second_of(p, pairs)
            pairs = shifted_pairs(q, 2)
            slope_z[1, pl.ds(REACH + i, GROUP)] = first_of(pairs)
            q_zz = second_of(q, pairs)
            pairs = shifted_pairs(p, 1)
            p_yy = second_of(p, pairs)
            if imaging:
                j = t // IMAGE_EVERY
                slopes[j, 1, rows] = first_of(pairs)
                slopes[j, 2, rows] = slope
            across = coef[1, rows] * p_zz + p_yy
            rotated = coef[0, rows] * q_zz
            base[0, rows] = (
                2.0 * p - p_old + inject[t, rows]
                + (coef[3, rows] * across + coef[4, rows] * rotated)
            )
            base[1, rows] = (
                2.0 * q - q_old + (coef[4, rows] * across + coef[5, rows] * rotated)
            )

    def after(t):
        imaging = t % IMAGE_EVERY == IMAGE_EVERY - 1
        last = t == STEPS - 1

        @pl.when(has_left)
        def _():
            halo_left(t).wait_send()
            halo_right(t).wait_recv()

        @pl.when(has_right)
        def _():
            halo_right(t).wait_send()
            halo_left(t).wait_recv()

        for start in (0, far):
            for f in range(2):
                rows = pl.ds(start, REACH)
                slope_z[f, rows] = first_of(shifted_pairs(pad[t, f, rows], 2))
        for i in range(0, nx, GROUP):
            rows = pl.ds(i, GROUP)
            middle = pl.ds(REACH + i, GROUP)
            pairs = row_pairs(pad, (t, 0), i)
            p_xx = second_of(pad[t, 0, middle], pairs)
            if imaging:
                slopes[t // IMAGE_EVERY, 0, rows] = first_of(pairs)
            q_xx = second_of(pad[t, 1, middle], row_pairs(pad, (t, 1), i))
            p_xz = first_of(row_pairs(slope_z, (0,), i))
            q_xz = first_of(row_pairs(slope_z, (1,), i))
            across = coef[0, rows] * p_xx - coef[2, rows] * p_xz
            rotated = coef[1, rows] * q_xx + coef[2, rows] * q_xz
            p_new = base[0, rows] + (coef[3, rows] * across + coef[4, rows] * rotated)
            q_new = base[1, rows] + (coef[4, rows] * across + coef[5, rows] * rotated)
            if last:
                final_ref[0, rows] = p_new
                final_ref[1, rows] = q_new
            else:
                pad[t + 1, 0, middle] = p_new
                pad[t + 1, 1, middle] = q_new
                if i == 0:
                    @pl.when(has_left)
                    def _():
                        halo_left(t + 1).start()

                if i + GROUP == nx:
                    @pl.when(has_right)
                    def _():
                        halo_right(t + 1).start()

    def angles(j):
        t = j * IMAGE_EVERY + IMAGE_EVERY - 1
        take_blocks(j)
        blocks = arrived[j].astype(jnp.float32)
        for c in range(4):
            snap[c] = blocks[:, c * nx : (c + 1) * nx]
        for x in range(nx):
            s, fx, fy, fz = (
                snap.at[c].reshape(ny * nx, nz)[pl.ds(x, ny, stride=nx), :] for c in range(4)
            )
            p = pad[t, 0, REACH + x]
            rate = p - pad[t - 1, 0, REACH + x]
            gx = -rate * slopes[j, 0, x]
            gy = -rate * slopes[j, 1, x]
            gz = -rate * slopes[j, 2, x]
            inner = fx * gx + fy * gy + fz * gz
            lengths = jnp.sqrt(fx * fx + fy * fy + fz * fz) * jnp.sqrt(gx * gx + gy * gy + gz * gz)
            cosine = inner / jnp.maximum(lengths, 1.0)
            aim[j, 0, x] = (cosine + 1.0) * (0.5 * (FINE - 1))
            aim[j, 1, x] = s * p

    before(0)
    after(0)
    before(1)
    stage(1)
    after(1)
    before(2)
    after(2)
    before(3)
    angles(0)
    after(3)
    angles(1)

    table = table_ref[...]
    lower = [
        jnp.sum((table < b).astype(jnp.float32), axis=1, keepdims=True) for b in range(NBIN + 1)
    ]
    for x in range(nx):
        uses = [(aim[j, 0, x], aim[j, 1, x]) for j in range(STEPS // IMAGE_EVERY)]
        above = [jnp.clip(u - lower[0] + 1.0, 0.0, 1.0) for u, _ in uses]
        for b in range(NBIN):
            beyond = [jnp.clip(u - lower[b + 1] + 1.0, 0.0, 1.0) for u, _ in uses]
            total = None
            for (_, w), low, high in zip(uses, above, beyond):
                term = (low - high) * w
                total = term if total is None else total + term
            images_ref[b, x] = total.astype(jnp.bfloat16)
            above = beyond
    sent_blocks(0)
    sent_blocks(1)


def local(
    n,
    wave_now,
    wave_prev,
    speed_term,
    thomsen_epsilon,
    thomsen_delta,
    tilt_angle,
    source_store,
    receiver_row,
    receiver_column,
    receiver_traces,
    angle_table,
):
    fields, nx, ny, nz = wave_now.shape
    snaps, parts, whole_x, local_ny, _ = source_store.shape
    padded_x = nx + 2 * REACH
    f32, bf16 = jnp.float32, jnp.bfloat16
    hbm = pl.BlockSpec(memory_space=pltpu.HBM)
    vmem = pl.BlockSpec(memory_space=pltpu.VMEM)
    return pl.pallas_call(
        functools.partial(kernel, n),
        out_shape=(
            jax.ShapeDtypeStruct((NBIN, nx, ny, nz), bf16),
            jax.ShapeDtypeStruct((fields, nx, ny, nz), f32),
        ),
        in_specs=[hbm] * 11,
        out_specs=(vmem, vmem),
        scratch_shapes=[
            pltpu.VMEM((STEPS, fields, padded_x, ny, nz), f32),
            pltpu.VMEM((fields, nx, ny, nz), f32),
            pltpu.VMEM((4, nx, ny, nz), f32),
            pltpu.VMEM((6, nx, ny, nz), f32),
            pltpu.VMEM((snaps, parts, local_ny, whole_x, nz), bf16),
            pltpu.VMEM((snaps, n, local_ny, parts * nx, nz), bf16),
            pltpu.VMEM((snaps, ny, parts * nx, nz), bf16),
            pltpu.VMEM((parts, ny, nx, nz), f32),
            pltpu.VMEM((snaps, 3, nx, ny, nz), f32),
            pltpu.VMEM((snaps, 2, nx, ny, nz), f32),
            pltpu.VMEM((STEPS, nx, ny, nz), f32),
            pltpu.VMEM((fields, nx, ny, nz), f32),
            pltpu.VMEM((fields, padded_x, ny, nz), f32),
            pltpu.VMEM((1, receiver_row.shape[0]), jnp.int32),
            pltpu.VMEM((1, receiver_row.shape[0]), jnp.int32),
            pltpu.VMEM(receiver_traces.shape, f32),
            pltpu.VMEM((1, angle_table.shape[0]), jnp.int32),
            pltpu.SemaphoreType.DMA((11,)),
            pltpu.SemaphoreType.DMA((STEPS, 2)),
            pltpu.SemaphoreType.DMA((STEPS, 2)),
            pltpu.SemaphoreType.DMA((snaps, n)),
            pltpu.SemaphoreType.DMA((snaps, n)),
        ],
        compiler_params=pltpu.CompilerParams(
            collective_id=0, has_side_effects=True, vmem_limit_bytes=62914560
        ),
    )(
        wave_now,
        wave_prev,
        speed_term,
        thomsen_epsilon,
        thomsen_delta,
        tilt_angle,
        source_store.transpose(0, 1, 3, 2, 4),
        receiver_row.reshape(1, -1),
        receiver_column.reshape(1, -1),
        receiver_traces,
        angle_table.reshape(1, -1),
    )


def solution(mesh):
    placed = (
        P("shot", "gx", None, None),
        P("shot", "gx", None, None),
        P("gx", None, None),
        P("gx", None, None),
        P("gx", None, None),
        P("gx", None, None),
        P("shot", None, None, "gx", None),
        P("shot"),
        P("shot"),
        P("shot", None),
        P(),
    )
    return jax.shard_map(
        functools.partial(local, mesh.shape["gx"]),
        mesh=mesh,
        in_specs=placed,
        out_specs=(P("shot", "gx", None, None), P("shot", "gx", None, None)),
        check_vma=False,
    )
```

```python
import functools

import jax
import jax.numpy as jnp
from jax import lax
from jax.experimental import pallas as pl
from jax.experimental.pallas import tpu as pltpu
from jax.sharding import PartitionSpec as P

STEPS = 4
IMAGE_EVERY = 2
NBIN = 8
FINE = 32
REC_DEPTH = 2
REACH = 4
GROUP = 4

second_coeffs = (-205.0 / 72.0, 8.0 / 5.0, -1.0 / 5.0, 8.0 / 315.0, -1.0 / 560.0)
first_coeffs = (4.0 / 5.0, -1.0 / 5.0, 4.0 / 105.0, -1.0 / 280.0)
MESH = pl.DeviceIdType.MESH


def shifted_pairs(f, axis):
    size = f.shape[axis]
    place = lax.broadcasted_iota(jnp.int32, f.shape, axis)
    pairs = []
    for k in range(1, REACH + 1):
        ahead = jnp.where(place < size - k, pltpu.roll(f, size - k, axis), 0.0)
        behind = jnp.where(place >= k, pltpu.roll(f, k, axis), 0.0)
        pairs.append((ahead, behind))
    return pairs


def second_of(f, pairs):
    total = second_coeffs[0] * f
    for k, (ahead, behind) in enumerate(pairs):
        total = total + second_coeffs[k + 1] * (ahead + behind)
    return total


def first_of(pairs):
    total = None
    for k, (ahead, behind) in enumerate(pairs):
        term = first_coeffs[k] * (ahead - behind)
        total = term if total is None else total + term
    return total


def row_pairs(ref, lead, start):
    return [
        (
            ref[lead + (pl.ds(start + REACH + k, GROUP),)],
            ref[lead + (pl.ds(start + REACH - k, GROUP),)],
        )
        for k in range(1, REACH + 1)
    ]


def kernel(
    n,
    now_hbm, prev_hbm, speed_hbm, eps_hbm, delta_hbm, tilt_hbm, source_hbm,
    rows_hbm, cols_hbm, traces_hbm, table_hbm,
    images_ref, final_ref,
    pad, prev, med, coef, source, staged, arrived, snap, slopes, aim, inject, base, slope_z,
    rows_ref, cols_ref, traces_ref, table_ref,
    in_sem, halo_send, halo_recv, all_send, all_recv,
):
    me = lax.axis_index("gx")
    nx, ny, nz = prev.shape[1:]
    local_ny = source.shape[2]
    has_left, has_right = me > 0, me < n - 1
    left, right = lax.rem(me + n - 1, n), lax.rem(me + 1, n)
    own = pl.ds(REACH, nx)
    far = REACH + nx

    barrier = pltpu.get_barrier_semaphore()

    def greet(k, carry):
        pl.semaphore_signal(
            barrier, inc=1, device_id={"gx": lax.rem(me + k, n)}, device_id_type=MESH
        )
        return carry

    lax.fori_loop(1, n, greet, 0)

    loads = [
        pltpu.make_async_copy(source_hbm, source, in_sem.at[0]),
        pltpu.make_async_copy(tilt_hbm, med.at[0], in_sem.at[1]),
        pltpu.make_async_copy(speed_hbm, med.at[1], in_sem.at[2]),
        pltpu.make_async_copy(eps_hbm, med.at[2], in_sem.at[3]),
        pltpu.make_async_copy(delta_hbm, med.at[3], in_sem.at[4]),
        pltpu.make_async_copy(rows_hbm, rows_ref, in_sem.at[7]),
        pltpu.make_async_copy(cols_hbm, cols_ref, in_sem.at[8]),
        pltpu.make_async_copy(traces_hbm, traces_ref, in_sem.at[9]),
        pltpu.make_async_copy(table_hbm, table_ref, in_sem.at[10]),
        pltpu.make_async_copy(now_hbm, pad.at[0, :, own], in_sem.at[5]),
        pltpu.make_async_copy(prev_hbm, prev, in_sem.at[6]),
    ]
    for load in loads:
        load.start()

    def halo_left(t):
        source_of = now_hbm.at[:, pl.ds(0, REACH)] if t == 0 else pad.at[t, :, pl.ds(REACH, REACH)]
        return pltpu.make_async_remote_copy(
            src_ref=source_of,
            dst_ref=pad.at[t, :, pl.ds(far, REACH)],
            send_sem=halo_send.at[t, 0],
            recv_sem=halo_recv.at[t, 1],
            device_id={"gx": left},
            device_id_type=MESH,
        )

    def halo_right(t):
        source_of = (
            now_hbm.at[:, pl.ds(nx - REACH, REACH)] if t == 0 else pad.at[t, :, pl.ds(nx, REACH)]
        )
        return pltpu.make_async_remote_copy(
            src_ref=source_of,
            dst_ref=pad.at[t, :, pl.ds(0, REACH)],
            send_sem=halo_send.at[t, 1],
            recv_sem=halo_recv.at[t, 0],
            device_id={"gx": right},
            device_id_type=MESH,
        )

    def block_to(j, k, target, slot):
        return pltpu.make_async_remote_copy(
            src_ref=staged.at[j, target],
            dst_ref=arrived.at[j, pl.ds(slot * local_ny, local_ny)],
            send_sem=all_send.at[j, k],
            recv_sem=all_recv.at[j, k],
            device_id={"gx": target},
            device_id_type=MESH,
        )

    def send_blocks(j):
        def send(k, carry):
            block_to(j, k, lax.rem(me + k, n), me).start()
            return carry

        lax.fori_loop(1, n, send, 0)
        arrived[j, pl.ds(me * local_ny, local_ny)] = staged[j, me]

    def take_blocks(j):
        def take(k, carry):
            block_to(j, k, lax.rem(me + k, n), lax.rem(me + n - k, n)).wait_recv()
            return carry

        lax.fori_loop(1, n, take, 0)

    def sent_blocks(j):
        def sent(k, carry):
            block_to(j, k, lax.rem(me + k, n), me).wait_send()
            return carry

        lax.fori_loop(1, n, sent, 0)

    for t in range(STEPS):
        @pl.when(me == 0)
        def _():
            pad[t, :, pl.ds(0, REACH)] = jnp.zeros((2, REACH, ny, nz), jnp.float32)

        @pl.when(me == n - 1)
        def _():
            pad[t, :, pl.ds(far, REACH)] = jnp.zeros((2, REACH, ny, nz), jnp.float32)

    for load in loads[1:9]:
        load.wait()
    for i in range(0, nx, GROUP):
        rows = pl.ds(i, GROUP)
        tilt = med[0, rows]
        cosine = jnp.cos(tilt)
        sine = jnp.sin(tilt)
        speed = med[1, rows]
        ratio = jnp.sqrt(1.0 + 2.0 * med[3, rows])
        coef[0, rows] = cosine * cosine
        coef[1, rows] = sine * sine
        coef[2, rows] = 2.0 * sine * cosine
        coef[3, rows] = speed * (1.0 + 2.0 * med[2, rows])
        coef[4, rows] = speed * ratio
        coef[5, rows] = speed

    first_row = me * nx
    at_column = cols_ref[...] == lax.broadcasted_iota(jnp.int32, (ny, cols_ref.shape[1]), 0)
    at_depth = lax.broadcasted_iota(jnp.int32, (ny, nz), 1) == REC_DEPTH

    def one_row(x, carry):
        here = jnp.where(rows_ref[...] == first_row + x, traces_ref[...], 0.0)
        for t in range(STEPS):
            summed = jnp.sum(
                jnp.where(at_column, here[t : t + 1], 0.0), axis=1, keepdims=True
            )
            inject[t, x] = jnp.where(at_depth, summed, 0.0)
        return carry

    lax.fori_loop(0, nx, one_row, 0)

    def stage(j):
        for y in range(local_ny):
            for c in range(4):
                snap[c, pl.ds(0, n)] = source[j, c, y].astype(jnp.float32).reshape(n, nx, nz)
            joined = jnp.concatenate([snap[c, pl.ds(0, n)] for c in range(4)], axis=1)
            staged[j, :, y] = joined.astype(jnp.bfloat16)
        send_blocks(j)

    for load in loads[9:]:
        load.wait()

    def before(t):
        imaging = t % IMAGE_EVERY == IMAGE_EVERY - 1
        for i in range(0, nx, GROUP):
            rows = pl.ds(i, GROUP)
            p = pad[t, 0, pl.ds(REACH + i, GROUP)]
            q = pad[t, 1, pl.ds(REACH + i, GROUP)]
            p_old = prev[0, rows] if t == 0 else pad[t - 1, 0, pl.ds(REACH + i, GROUP)]
            q_old = prev[1, rows] if t == 0 else pad[t - 1, 1, pl.ds(REACH + i, GROUP)]
            pairs = shifted_pairs(p, 2)
            slope = first_of(pairs)
            slope_z[0, pl.ds(REACH + i, GROUP)] = slope
            p_zz = second_of(p, pairs)
            pairs = shifted_pairs(q, 2)
            slope_z[1, pl.ds(REACH + i, GROUP)] = first_of(pairs)
            q_zz = second_of(q, pairs)
            pairs = shifted_pairs(p, 1)
            p_yy = second_of(p, pairs)
            if imaging:
                j = t // IMAGE_EVERY
                slopes[j, 1, rows] = first_of(pairs)
                slopes[j, 2, rows] = slope
            across = coef[1, rows] * p_zz + p_yy
            rotated = coef[0, rows] * q_zz
            base[0, rows] = (
                2.0 * p - p_old + inject[t, rows]
                + (coef[3, rows] * across + coef[4, rows] * rotated)
            )
            base[1, rows] = (
                2.0 * q - q_old + (coef[4, rows] * across + coef[5, rows] * rotated)
            )

    def after(t):
        imaging = t % IMAGE_EVERY == IMAGE_EVERY - 1
        last = t == STEPS - 1

        @pl.when(has_left)
        def _():
            halo_left(t).wait_send()
            halo_right(t).wait_recv()

        @pl.when(has_right)
        def _():
            halo_right(t).wait_send()
            halo_left(t).wait_recv()

        for start in (0, far):
            for f in range(2):
                rows = pl.ds(start, REACH)
                slope_z[f, rows] = first_of(shifted_pairs(pad[t, f, rows], 2))
        for i in range(0, nx, GROUP):
            rows = pl.ds(i, GROUP)
            middle = pl.ds(REACH + i, GROUP)
            pairs = row_pairs(pad, (t, 0), i)
            p_xx = second_of(pad[t, 0, middle], pairs)
            if imaging:
                slopes[t // IMAGE_EVERY, 0, rows] = first_of(pairs)
            q_xx = second_of(pad[t, 1, middle], row_pairs(pad, (t, 1), i))
            p_xz = first_of(row_pairs(slope_z, (0,), i))
            q_xz = first_of(row_pairs(slope_z, (1,), i))
            across = coef[0, rows] * p_xx - coef[2, rows] * p_xz
            rotated = coef[1, rows] * q_xx + coef[2, rows] * q_xz
            p_new = base[0, rows] + (coef[3, rows] * across + coef[4, rows] * rotated)
            q_new = base[1, rows] + (coef[4, rows] * across + coef[5, rows] * rotated)
            if last:
                final_ref[0, rows] = p_new
                final_ref[1, rows] = q_new
            else:
                pad[t + 1, 0, middle] = p_new
                pad[t + 1, 1, middle] = q_new
                if i == 0:
                    @pl.when(has_left)
                    def _():
                        halo_left(t + 1).start()

                if i + GROUP == nx:
                    @pl.when(has_right)
                    def _():
                        halo_right(t + 1).start()

    def angles(j):
        t = j * IMAGE_EVERY + IMAGE_EVERY - 1
        take_blocks(j)
        blocks = arrived[j].astype(jnp.float32)
        for c in range(4):
            snap[c] = blocks[:, c * nx : (c + 1) * nx]
        for x in range(nx):
            s, fx, fy, fz = (
                snap.at[c].reshape(ny * nx, nz)[pl.ds(x, ny, stride=nx), :] for c in range(4)
            )
            p = pad[t, 0, REACH + x]
            rate = p - pad[t - 1, 0, REACH + x]
            gx = -rate * slopes[j, 0, x]
            gy = -rate * slopes[j, 1, x]
            gz = -rate * slopes[j, 2, x]
            inner = fx * gx + fy * gy + fz * gz
            lengths = jnp.sqrt(fx * fx + fy * fy + fz * fz) * jnp.sqrt(gx * gx + gy * gy + gz * gz)
            cosine = inner / jnp.maximum(lengths, 1.0)
            aim[j, 0, x] = (cosine + 1.0) * (0.5 * (FINE - 1))
            aim[j, 1, x] = s * p

    before(0)
    pl.semaphore_wait(barrier, n - 1)

    @pl.when(has_left)
    def _():
        halo_left(0).start()

    @pl.when(has_right)
    def _():
        halo_right(0).start()

    loads[0].wait()
    stage(0)
    after(0)
    before(1)
    stage(1)
    after(1)
    before(2)
    after(2)
    before(3)
    angles(0)
    after(3)
    angles(1)

    table = table_ref[...]
    lower = [
        jnp.sum((table < b).astype(jnp.float32), axis=1, keepdims=True) for b in range(NBIN + 1)
    ]
    for x in range(nx):
        uses = [(aim[j, 0, x], aim[j, 1, x]) for j in range(STEPS // IMAGE_EVERY)]
        above = [jnp.clip(u - lower[0] + 1.0, 0.0, 1.0) for u, _ in uses]
        for b in range(NBIN):
            beyond = [jnp.clip(u - lower[b + 1] + 1.0, 0.0, 1.0) for u, _ in uses]
            total = None
            for (_, w), low, high in zip(uses, above, beyond):
                term = (low - high) * w
                total = term if total is None else total + term
            images_ref[b, x] = total.astype(jnp.bfloat16)
            above = beyond
    sent_blocks(0)
    sent_blocks(1)


def local(
    n,
    wave_now,
    wave_prev,
    speed_term,
    thomsen_epsilon,
    thomsen_delta,
    tilt_angle,
    source_store,
    receiver_row,
    receiver_column,
    receiver_traces,
    angle_table,
):
    fields, nx, ny, nz = wave_now.shape
    snaps, parts, whole_x, local_ny, _ = source_store.shape
    padded_x = nx + 2 * REACH
    f32, bf16 = jnp.float32, jnp.bfloat16
    hbm = pl.BlockSpec(memory_space=pltpu.HBM)
    vmem = pl.BlockSpec(memory_space=pltpu.VMEM)
    return pl.pallas_call(
        functools.partial(kernel, n),
        out_shape=(
            jax.ShapeDtypeStruct((NBIN, nx, ny, nz), bf16),
            jax.ShapeDtypeStruct((fields, nx, ny, nz), f32),
        ),
        in_specs=[hbm] * 11,
        out_specs=(vmem, vmem),
        scratch_shapes=[
            pltpu.VMEM((STEPS, fields, padded_x, ny, nz), f32),
            pltpu.VMEM((fields, nx, ny, nz), f32),
            pltpu.VMEM((4, nx, ny, nz), f32),
            pltpu.VMEM((6, nx, ny, nz), f32),
            pltpu.VMEM((snaps, parts, local_ny, whole_x, nz), bf16),
            pltpu.VMEM((snaps, n, local_ny, parts * nx, nz), bf16),
            pltpu.VMEM((snaps, ny, parts * nx, nz), bf16),
            pltpu.VMEM((parts, ny, nx, nz), f32),
            pltpu.VMEM((snaps, 3, nx, ny, nz), f32),
            pltpu.VMEM((snaps, 2, nx, ny, nz), f32),
            pltpu.VMEM((STEPS, nx, ny, nz), f32),
            pltpu.VMEM((fields, nx, ny, nz), f32),
            pltpu.VMEM((fields, padded_x, ny, nz), f32),
            pltpu.VMEM((1, receiver_row.shape[0]), jnp.int32),
            pltpu.VMEM((1, receiver_row.shape[0]), jnp.int32),
            pltpu.VMEM(receiver_traces.shape, f32),
            pltpu.VMEM((1, angle_table.shape[0]), jnp.int32),
            pltpu.SemaphoreType.DMA((11,)),
            pltpu.SemaphoreType.DMA((STEPS, 2)),
            pltpu.SemaphoreType.DMA((STEPS, 2)),
            pltpu.SemaphoreType.DMA((snaps, n)),
            pltpu.SemaphoreType.DMA((snaps, n)),
        ],
        compiler_params=pltpu.CompilerParams(
            collective_id=0, has_side_effects=True, vmem_limit_bytes=62914560
        ),
    )(
        wave_now,
        wave_prev,
        speed_term,
        thomsen_epsilon,
        thomsen_delta,
        tilt_angle,
        source_store.transpose(0, 1, 3, 2, 4),
        receiver_row.reshape(1, -1),
        receiver_column.reshape(1, -1),
        receiver_traces,
        angle_table.reshape(1, -1),
    )


def solution(mesh):
    placed = (
        P("shot", "gx", None, None),
        P("shot", "gx", None, None),
        P("gx", None, None),
        P("gx", None, None),
        P("gx", None, None),
        P("gx", None, None),
        P("shot", None, None, "gx", None),
        P("shot"),
        P("shot"),
        P("shot", None),
        P(),
    )
    return jax.shard_map(
        functools.partial(local, mesh.shape["gx"]),
        mesh=mesh,
        in_specs=placed,
        out_specs=(P("shot", "gx", None, None), P("shot", "gx", None, None)),
        check_vma=False,
    )
```
